256 devices in a mesh: blk: 128 (over z_hi, y, x, core), rep: 2 (over z_lo).
Axes of the slice: x: 4, y: 4, z: 8 (z_hi: 4, z_lo: 2; z = z_hi * 2 + z_lo), core: 2. Of those that a mesh axis runs over, the one named last changes fastest.
Arguments:
- fwd_in: bfloat16 [114688, 1024], P(('blk', 'rep')), may hold values from -6 to 6
- bwd_in: bfloat16 [114688, 1024], P(('blk', 'rep')), may hold values from -6 to 6
- cotangent: bfloat16 [114688, 1024], P(('blk', 'rep')), may hold values from -6 to 6
- w_in: bfloat16 [1024, 65536], P(None, 'blk'), may hold values from -0.1875 to 0.1875
- w_out: bfloat16 [65536, 1024], P('blk'), may hold values from -0.125 to 0.125
Outputs:
- forward_out: bfloat16 [114688, 1024], P(('blk', 'rep'))
- input_grad: bfloat16 [114688, 1024], P(('blk', 'rep'))
- in_grad: float32 [1024, 65536], P('rep', 'blk')
- down_grad: float32 [65536, 1024], P('blk', 'rep')
The draws below stay inside these ranges and needn't reach their ends.
All inputs are finite; a program needn't handle non-finite values.
Results may differ from the reference program's by a relative error of at most 0.0066.
Values may be sent and summed in bfloat16 or wider, within the bound.
A program may use at most 128 MiB of HBM per device.

```python
import jax
import jax.numpy as jnp
from jax import lax

D = 1024
HID_DEV = 512
TICKS = 4
MB_DEV = 448
FF = 65536
ROWS = 114688
N_BLK = 128
N_REP = 2


def steps_of(rng, extent, pieces, smallest, high):
    def one(dim, blocks):
        steps = jax.random.uniform(jax.random.fold_in(jax.random.fold_in(rng, 6), dim), (blocks,), jnp.float32, smallest / len(pieces), high / len(pieces))
        return jnp.repeat(jnp.exp(steps), extent[dim] // blocks).reshape((-1,) + (1,) * (len(extent) - dim - 1))

    loudness = one(*pieces[0])
    for cut in pieces[1:]:
        loudness = loudness * one(*cut)
    return loudness


def noise(key, dims, scale, reach, split=(), kind=jnp.bfloat16):
    result = jax.random.normal(key, dims, jnp.float32) * scale
    if len(split) > 0:
        result = steps_of(key, dims, split, -0.22, 0.18) * result
    return jnp.clip(result, min=-reach, max=reach).astype(kind)


def setup_inputs(seed: int = 0) -> dict:
    key_list = jax.random.split(jax.random.key(seed), 6)
    return {
        "fwd_in": noise(key_list[0], (ROWS, D), 1.0, 6.0, ((0, 256),)),
        "bwd_in": noise(key_list[1], (ROWS, D), 1.0, 6.0, ((0, 256),)),
        "cotangent": noise(key_list[2], (ROWS, D), 1.0, 6.0, ((0, 256),)),
        "w_in": noise(key_list[3], (D, FF), D ** -0.5, 0.1875, ((1, 128),)),
        "w_out": noise(key_list[4], (FF, D), (TICKS * HID_DEV) ** -0.5, 0.125, ((0, 128),)),
    }


def inner(left, right, left_dim, right_dim):
    return lax.dot_general(left, right, (((left_dim,), (right_dim,)), ((), ())), preferred_element_type=jnp.float32)

def slot_pair(w_in, w_out, holder):
    offset = (holder * HID_DEV).astype(jnp.int32)
    return (lax.dynamic_slice_in_dim(w_in, offset, HID_DEV, 1), lax.dynamic_slice_in_dim(w_out, offset, HID_DEV, 0))

def backward_pieces(inputs, cotan, w_in_slot, w_out_slot):
    preact = jnp.dot(inputs, w_in_slot, preferred_element_type=jnp.float32)
    active, pullback = jax.vjp(jax.nn.gelu, preact)
    hidden = active.astype(jnp.bfloat16)
    hid_grad = inner(cotan, w_out_slot, 1, 1)
    pre_grad = pullback(hid_grad)[0].astype(jnp.bfloat16)
    return (hidden, pre_grad)

def reference(fwd_in, bwd_in, cotangent, w_in, w_out):
    span_rows = MB_DEV * N_REP

    def take_block(array, block):
        offset = (block * span_rows).astype(jnp.int32)
        return lax.dynamic_slice_in_dim(array, offset, span_rows, 0)

    def per_block(block):
        fwd_rows = take_block(fwd_in, block)
        bwd_rows = take_block(bwd_in, block)
        cot_rows = take_block(cotangent, block)
        fwd_sum = jnp.zeros((span_rows, D), jnp.float32)
        grad_sum = jnp.zeros((span_rows, D), jnp.float32)
        for tick in range(TICKS):
            holder = ((block + N_BLK - tick) % N_BLK).astype(jnp.int32)
            w_in_slot, w_out_slot = slot_pair(w_in, w_out, holder)
            preact = jnp.dot(fwd_rows, w_in_slot, preferred_element_type=jnp.float32)
            fwd_sum = fwd_sum + jnp.dot(jax.nn.gelu(preact).astype(jnp.bfloat16), w_out_slot, preferred_element_type=jnp.float32)
            hidden, pre_grad = backward_pieces(bwd_rows, cot_rows, w_in_slot, w_out_slot)
            grad_sum = grad_sum + inner(pre_grad, w_in_slot, 1, 1)
        return (fwd_sum.astype(jnp.bfloat16), grad_sum.astype(jnp.bfloat16))

    def per_holder(holder):
        w_in_slot, w_out_slot = slot_pair(w_in, w_out, holder)
        in_sum = jnp.zeros((D, HID_DEV), jnp.float32)
        out_sum = jnp.zeros((HID_DEV, D), jnp.float32)
        for tick in range(TICKS):
            block = ((holder + tick) % N_BLK).astype(jnp.int32)
            bwd_rows = take_block(bwd_in, block)
            cot_rows = take_block(cotangent, block)
            hidden, pre_grad = backward_pieces(bwd_rows, cot_rows, w_in_slot, w_out_slot)
            in_sum = in_sum + inner(bwd_rows, pre_grad, 0, 0)
            out_sum = out_sum + inner(hidden, cot_rows, 0, 0)
        return (in_sum, out_sum)
    blocks = jnp.arange(N_BLK, dtype=jnp.int32)
    fwd_parts, grad_parts = lax.map(per_block, blocks)
    in_parts, out_parts = lax.map(per_holder, blocks)
    forward_out = fwd_parts.reshape(-1, D)
    input_grad = grad_parts.reshape(-1, D)
    in_grad = jnp.transpose(in_parts, (1, 0, 2)).reshape(D, N_BLK * HID_DEV)
    down_grad = out_parts.reshape(N_BLK * HID_DEV, D)
    return (forward_out, input_grad, in_grad, down_grad)
```

```python
import jax
import jax.numpy as jnp
from jax import lax
from jax.experimental import pallas as pl
from jax.experimental.pallas import tpu as pltpu
from jax.sharding import PartitionSpec as P

MESH = pl.DeviceIdType.MESH
MB, D, HID, CH = 448, 1024, 512, 128
HALF = HID // 2
F32, BF16 = jnp.float32, jnp.bfloat16
SQ = 0.7978845608028654

P1C0, P2C0, P3C0, P1C1, P2C1, P3C1 = range(6)


def inner(left, right, left_dim, right_dim):
    return lax.dot_general(
        left, right, (((left_dim,), (right_dim,)), ((), ())), preferred_element_type=F32
    )


def kernel(
    fwd_hbm, bwd_hbm, cot_hbm, win_hbm, wout_hbm,
    fout, iout, inout, downout,
    tok, w_i, w_o, facc, iacc, orecv, grad, own_send, gs, p1sum, keep, final, g3,
    rly_i, rly_o, rly_b,
    loc_sem, wx_send, wx_recv, tok_send, tok_recv,
    xp_send, xp_recv, rf_send, rf_recv,
    own_sem, fin_sem, xm_send, g3_sem, rb_send, rb_recv, out_send, out_recv,
):
    blk, rep = lax.axis_index("blk"), lax.axis_index("rep")
    core = lax.rem(blk, 2)
    chip = lax.div(blk, 2)
    pos = lax.rem(chip, 16)
    zhi = lax.div(chip, 16)
    other, orep = 1 - core, 1 - rep

    def at(chip_, core_, rep_):
        return (lax.rem(chip_ + 64, 64) * 2 + core_, rep_)

    def corner(p):
        return pos == p

    def in_plane(p, core_=core):
        return at(zhi * 16 + p, core_, rep)

    def remote(src, dst, ssem, rsem, dev):
        return pltpu.make_async_remote_copy(
            src_ref=src, dst_ref=dst, send_sem=ssem, recv_sem=rsem,
            device_id=dev, device_id_type=MESH,
        )

    peer = at(chip, other, rep)
    ahead = at(chip + 1, core, rep)
    SRC_F, SRC_B = 15, 0

    def local_w(q):
        cols = pl.ds(pl.multiple_of(core * HALF + q * CH, CH), CH)
        return (
            pltpu.make_async_copy(win_hbm.at[:, cols], w_i.at[2 * core + q], loc_sem.at[3 + q]),
            pltpu.make_async_copy(wout_hbm.at[cols, :], w_o.at[2 * core + q], loc_sem.at[5 + q]),
        )

    toks = (fwd_hbm, bwd_hbm, cot_hbm)
    local_t = [pltpu.make_async_copy(toks[t], tok.at[t, core], loc_sem.at[t]) for t in range(3)]
    for q in range(2):
        for copy in local_w(q):
            copy.start()
    for copy in local_t:
        copy.start()

    barrier = pltpu.get_barrier_semaphore()

    def greet(dev):
        pl.semaphore_signal(barrier, inc=1, device_id=dev, device_id_type=MESH)

    greet(peer)
    for core_ in range(2):
        greet(at(chip, core_, orep))
        for rep_ in range(2):
            greet(at(chip + 1, core_, rep_))
            greet(at(chip - 1, core_, rep_))
    for p in (0, 3, 12, 15):
        @pl.when(corner(p))
        def _():
            for other_p in (0, 3, 12, 15):
                if other_p != p:
                    greet(in_plane(other_p))
    is_corner = corner(0) | corner(3) | corner(12) | corner(15)

    @pl.when(jnp.logical_not(is_corner))
    def _():
        pl.semaphore_wait(barrier, 11)

    @pl.when(is_corner)
    def _():
        pl.semaphore_wait(barrier, 14)

    def swap_w(q):
        cols = pl.ds(pl.multiple_of(other * HALF + q * CH, CH), CH)
        return (
            remote(win_hbm.at[:, cols], w_i.at[2 * core + q], wx_send.at[q, 0], wx_recv.at[q, 0], peer),
            remote(wout_hbm.at[cols, :], w_o.at[2 * core + q], wx_send.at[q, 1], wx_recv.at[q, 1], peer),
        )

    swaps = [copy for q in range(2) for copy in swap_w(q)]
    for copy in swaps:
        copy.start()
    swap_t = [
        remote(toks[t], tok.at[t, core], tok_send.at[t], tok_recv.at[t], peer) for t in range(3)
    ]
    for copy in swap_t:
        copy.start()

    def arrived_w(q):
        return (
            pltpu.make_async_remote_copy(
                src_ref=w_i.at[2 * other + q], dst_ref=w_i.at[2 * other + q],
                send_sem=wx_send.at[q, 0], recv_sem=wx_recv.at[q, 0],
                device_id=peer, device_id_type=MESH),
            pltpu.make_async_remote_copy(
                src_ref=w_o.at[2 * other + q], dst_ref=w_o.at[2 * other + q],
                send_sem=wx_send.at[q, 1], recv_sem=wx_recv.at[q, 1],
                device_id=peer, device_id_type=MESH),
        )

    def piece_w(ref_i, ref_o, n, s):
        if s < 2:
            return ref_i.at[n, pl.ds(s * 512, 512)]
        return ref_o.at[n, pl.ds((s - 2) * 64, 64)]

    RELAY_F = {1: 0, 2: 12, 3: 3}
    RELAY_B = {1: 15, 2: 3, 3: 12}

    def rly_w(i, s):
        return rly_i.at[i] if s == 1 else rly_o.at[i]

    def whole_w(i, n):
        return (
            remote(w_i.at[n], w_i.at[4 + i], xp_send.at[i, 0], xp_recv.at[i, 0], ahead),
            remote(w_o.at[n], w_o.at[4 + i], xp_send.at[i, 1], xp_recv.at[i, 1], ahead),
        )

    def send_w(i, n):
        @pl.when(jnp.logical_not(corner(SRC_F)))
        def _():
            for copy in whole_w(i, n):
                copy.start()

        @pl.when(corner(SRC_F))
        def _():
            for s in (1, 2, 3):
                remote(piece_w(w_i, w_o, n, s), rly_w(i, s), xp_send.at[i, s // 2], rf_recv.at[i],
                       in_plane(RELAY_F[s])).start()
            remote(piece_w(w_i, w_o, n, 0), piece_w(w_i, w_o, 4 + i, 0), xp_send.at[i, 0],
                   xp_recv.at[i, 0], ahead).start()

    def pass_w(i):
        dev = at((zhi + 1) * 16, core, rep)
        for s, p in RELAY_F.items():
            @pl.when(corner(p))
            def _():
                copy = remote(rly_w(i, s), piece_w(w_i, w_o, 4 + i, s), rf_send.at[i],
                              xp_recv.at[i, s // 2], dev)
                remote(rly_w(i, s), rly_w(i, s), rf_send.at[i], rf_recv.at[i], dev).wait_recv()
                copy.start()

    def passed_w(i):
        for s, p in RELAY_F.items():
            @pl.when(corner(p))
            def _():
                remote(rly_w(i, s), rly_w(i, s), rf_send.at[i], rf_recv.at[i], ahead).wait_send()

    def place_g(i, h):
        q, kind = i // 3, i % 3 + 1
        if kind == 3:
            return g3.at[q, h], g3_sem.at[q], core, rep
        return final.at[1, rep, core, q], fin_sem.at[1, rep, core, q], 2 - kind, h

    def piece_g(ref, s):
        return ref.at[s // 2, pl.ds((s % 2) * 64, 64)]

    def send_g(i):
        for h in range(2):
            dst, sem, core_, rep_ = place_g(i, h)
            dev = at(chip - 1, core_, rep_)

            @pl.when(jnp.logical_not(corner(SRC_B)))
            def _():
                remote(gs.at[i, h], dst, xm_send.at[i, h], sem, dev).start()

            @pl.when(corner(SRC_B))
            def _():
                for s in (1, 2, 3):
                    remote(piece_g(gs.at[i, h], s), rly_b.at[i, h], xm_send.at[i, h],
                           rb_recv.at[i, h], in_plane(RELAY_B[s])).start()
                remote(piece_g(gs.at[i, h], 0), piece_g(dst, 0), xm_send.at[i, h], sem, dev).start()

    def pass_g(i):
        for s, p in RELAY_B.items():
            @pl.when(corner(p))
            def _():
                for h in range(2):
                    dst, sem, core_, rep_ = place_g(i, h)
                    dev = at(zhi * 16 - 1, core_, rep_)
                    copy = remote(rly_b.at[i, h], piece_g(dst, s), rb_send.at[i, h], sem, dev)
                    remote(rly_b.at[i, h], rly_b.at[i, h], rb_send.at[i, h], rb_recv.at[i, h],
                           dev).wait_recv()
                    copy.start()

    def passed_g(i):
        for s, p in RELAY_B.items():
            @pl.when(corner(p))
            def _():
                for h in range(2):
                    remote(rly_b.at[i, h], rly_b.at[i, h], rb_send.at[i, h], rb_recv.at[i, h],
                           ahead).wait_send()

    def compute(n, lo, hi):
        grad[...] = jnp.zeros_like(grad)

        def block(b, carry):
            wi, wo = w_i[n], w_o[n]
            pre = jnp.dot(tok[0, b], wi, preferred_element_type=F32)
            hid = (0.5 * pre * (1.0 + jnp.tanh(SQ * (pre + 0.044715 * (pre * pre * pre))))).astype(BF16)
            facc[b] += jnp.dot(hid, wo, preferred_element_type=F32)
            pre = jnp.dot(tok[1, b], wi, preferred_element_type=F32)
            hid_grad = inner(tok[2, b], wo, 1, 1)
            square = pre * pre
            t = jnp.tanh(SQ * (pre + 0.044715 * (square * pre)))
            cdf = 0.5 * (1.0 + t)
            slope = cdf + pre * (0.5 * (1.0 - t * t)) * (SQ * (1.0 + 3 * 0.044715 * square))
            hid = (pre * cdf).astype(BF16)
            pre_grad = (hid_grad * slope).astype(BF16)
            iacc[b] += inner(pre_grad, wi, 1, 1)
            grad[0] += inner(pre_grad, tok[1, b], 0, 0)
            grad[1] += inner(hid, tok[2, b], 0, 0)
            return carry

        lax.fori_loop(lo, hi, block, 0)

    def halves(ref, h):
        return ref[:, :, pl.ds(h * 512, 512)]

    for q in range(2):
        for copy in local_w(q):
            copy.wait()
        for copy in arrived_w(q):
            copy.wait_recv()
        if q == 0:
            send_w(P1C0, 2)
            send_w(P2C0, 0)
    facc[...] = jnp.zeros_like(facc)
    iacc[...] = jnp.zeros_like(iacc)
    for t in range(3):
        local_t[t].wait()
    for t in range(3):
        remote(toks[t], tok.at[t, other], tok_send.at[t], tok_recv.at[t], peer).wait_recv()

    def own_copy(n, h):
        j, q = lax.div(n, 2), lax.rem(n, 2)
        return remote(own_send.at[n, h], final.at[0, rep, core, q], own_sem.at[n, h],
                      fin_sem.at[0, rep, core, q], at(chip, j, h))

    def own_step(n, carry):
        j, q = lax.div(n, 2), lax.rem(n, 2)
        compute(n, j, 2)
        for h in range(2):
            mine = (core == j) & (rep == h)

            @pl.when(mine)
            def _():
                keep[q] = halves(grad, h)

            @pl.when(jnp.logical_not(mine))
            def _():
                own_send[n, h] = halves(grad, h).astype(BF16)
                own_copy(n, h).start()
        return carry

    lax.fori_loop(0, 4, own_step, 0)

    def finish_p1(q):
        for h in range(2):
            if h == 0:
                remote(g3.at[q], g3.at[q], xm_send.at[0, 0], g3_sem.at[q], ahead).wait_recv()
            gs[3 * q, h] = (halves(p1sum.at[q], h) + g3[q, h].astype(F32)).astype(BF16)
        send_g(3 * q)

    for i in range(6):
        q, kind = i // 3, i % 3 + 1
        pass_w(i)
        for copy in whole_w(i, 4 + i):
            copy.wait_recv()
        if kind == 1:
            send_w(3 * q + 2, 4 + i)
            if q == 0:
                send_w(P1C1, 3)
                send_w(P2C1, 1)
        compute(4 + i, 0, 1 if kind == 3 else 2)
        if kind == 1:
            p1sum[q] = grad[...]
        else:
            for h in range(2):
                gs[i, h] = halves(grad, h).astype(BF16)
            send_g(i)
        if i == 2:
            pass_g(P2C0)
        if i == 3:
            pass_g(P3C0)
            finish_p1(0)
        if i == 4:
            pass_g(P1C0)

    outs = [
        remote(acc.at[other], orecv.at[a], out_send.at[a], out_recv.at[a], peer)
        for a, acc in enumerate((facc, iacc))
    ]
    for copy in outs:
        copy.start()
    pass_g(P2C1)
    pass_g(P3C1)
    finish_p1(1)

    for a, (acc, out) in enumerate(((facc, fout), (iacc, iout))):
        outs[a].wait_recv()
        out[...] = (acc[core] + orecv[a]).astype(BF16)

    def arrived(side, rep_, core_, q):
        ref = final.at[side, rep_, core_, q]
        remote(ref, ref, xm_send.at[0, 0], fin_sem.at[side, rep_, core_, q], ahead).wait_recv()
        return ref[...].astype(F32)

    def finish(q):
        for core_ in (core, other):
            total = keep[q] if core_ is core else arrived(0, rep, core_, q)
            total = total + arrived(0, orep, core_, q)
            total = total + arrived(1, rep, core_, q)
            total = total + arrived(1, orep, core_, q)
            at_hid = pl.multiple_of(core_ * HALF + q * CH, CH)
            inout[:, pl.ds(at_hid, CH)] = total[0].T
            downout[pl.ds(at_hid, CH), :] = total[1]

    finish(0)
    pass_g(P1C1)
    finish(1)

    for copy in swaps + swap_t + outs:
        copy.wait_send()
    for i in range(6):
        for copy in whole_w(i, 4 + i):
            copy.wait_send()
        passed_w(i)
        passed_g(i)
        for h in range(2):
            remote(gs.at[i, h], gs.at[i, h], xm_send.at[i, h], g3_sem.at[0], ahead).wait_send()
    for n in range(4):
        for h in range(2):
            @pl.when(jnp.logical_not((core == n // 2) & (rep == h)))
            def _():
                own_copy(n, h).wait_send()


def on_device(fwd_in, bwd_in, cotangent, w_in, w_out):
    dma = pltpu.SemaphoreType.DMA
    vmem = pltpu.VMEM
    return pl.pallas_call(
        kernel,
        out_shape=(
            jax.ShapeDtypeStruct((MB, D), BF16),
            jax.ShapeDtypeStruct((MB, D), BF16),
            jax.ShapeDtypeStruct((HID, HID), F32),
            jax.ShapeDtypeStruct((HID, HID), F32),
        ),
        in_specs=[pl.BlockSpec(memory_space=pl.ANY)] * 5,
        out_specs=[pl.BlockSpec(memory_space=pltpu.VMEM)] * 4,
        scratch_shapes=[
            vmem((3, 2, MB, D), BF16),
            vmem((10, D, CH), BF16),
            vmem((10, CH, D), BF16),
            vmem((2, MB, D), F32),
            vmem((2, MB, D), F32),
            vmem((2, MB, D), F32),
            vmem((2, CH, D), F32),
            vmem((4, 2, 2, CH, 512), BF16),
            vmem((6, 2, 2, CH, 512), BF16),
            vmem((2, 2, CH, D), F32),
            vmem((2, 2, CH, 512), F32),
            vmem((2, 2, 2, 2, 2, CH, 512), BF16),
            vmem((2, 2, 2, CH, 512), BF16),
            vmem((6, 512, CH), BF16),
            vmem((6, 64, D), BF16),
            vmem((6, 2, 64, 512), BF16),
            dma((7,)),
            dma((2, 2)),
            dma((2, 2)),
            dma((3,)),
            dma((3,)),
            dma((6, 2)),
            dma((6, 2)),
            dma((6,)),
            dma((6,)),
            dma((4, 2)),
            dma((2, 2, 2, 2)),
            dma((6, 2)),
            dma((2,)),
            dma((6, 2)),
            dma((6, 2)),
            dma((2,)),
            dma((2,)),
        ],
        compiler_params=pltpu.CompilerParams(
            collective_id=0, has_side_effects=True, vmem_limit_bytes=60 * 2**20
        ),
        cost_estimate=pl.CostEstimate(
            flops=13_153_337_344, bytes_accessed=12 * 2**20, transcendentals=2 * 4 * MB * HID
        ),
    )(fwd_in, bwd_in, cotangent, w_in, w_out)


def solution(mesh):
    in_specs = (
        P(("blk", "rep"), None),
        P(("blk", "rep"), None),
        P(("blk", "rep"), None),
        P(None, "blk"),
        P("blk", None),
    )
    out_specs = (P(("blk", "rep"), None), P(("blk", "rep"), None), P("rep", "blk"), P("blk", "rep"))
    return jax.shard_map(
        on_device, mesh=mesh, in_specs=in_specs, out_specs=out_specs, check_vma=False
    )
```

```python
import jax
import jax.numpy as jnp
from jax import lax
from jax.experimental import pallas as pl
from jax.experimental.pallas import tpu as pltpu
from jax.sharding import PartitionSpec as P

MESH = pl.DeviceIdType.MESH
MB, D, HID, CH = 448, 1024, 512, 128
HALF = HID // 2
F32, BF16 = jnp.float32, jnp.bfloat16
SQ = 0.7978845608028654

P1C0, P1C1, P3C0, P2C0, P3C1, P2C1 = range(6)
KIND, CHUNK = (1, 1, 3, 2, 3, 2), (0, 1, 0, 0, 1, 1)


def inner(left, right, left_dim, right_dim):
    return lax.dot_general(
        left, right, (((left_dim,), (right_dim,)), ((), ())), preferred_element_type=F32
    )


def kernel(
    fwd_hbm, bwd_hbm, cot_hbm, win_hbm, wout_hbm,
    fout, iout, inout, downout,
    tok, w_i, w_o, facc, iacc, orecv, grad, own_send, gs, hold, zs, zr, keep, final, g3,
    p1full, ownfull, lrecv,
    rly_i, rly_o, rly_b,
    loc_sem, wx_send, wx_recv, tok_send, tok_recv,
    xp_send, xp_recv, xd_send, rf_send, rf_recv,
    own_sem, fin_sem, xm_send, g3_sem, z_send, z_recv, rb_send, rb_recv, out_send, out_recv, l_sem,
):
    blk, rep = lax.axis_index("blk"), lax.axis_index("rep")
    core = lax.rem(blk, 2)
    chip = lax.div(blk, 2)
    pos = lax.rem(chip, 16)
    zhi = lax.div(chip, 16)
    other, orep = 1 - core, 1 - rep

    def at(chip_, core_, rep_):
        return (lax.rem(chip_ + 64, 64) * 2 + core_, rep_)

    def corner(p):
        return pos == p

    def in_plane(p, core_=core):
        return at(zhi * 16 + p, core_, rep)

    def remote(src, dst, ssem, rsem, dev):
        return pltpu.make_async_remote_copy(
            src_ref=src, dst_ref=dst, send_sem=ssem, recv_sem=rsem,
            device_id=dev, device_id_type=MESH,
        )

    peer = at(chip, other, rep)
    ahead = at(chip + 1, core, rep)
    SRC_F, SRC_B = 15, 0

    def local_w(q):
        cols = pl.ds(pl.multiple_of(core * HALF + q * CH, CH), CH)
        return (
            pltpu.make_async_copy(win_hbm.at[:, cols], w_i.at[2 * core + q], loc_sem.at[3 + q]),
            pltpu.make_async_copy(wout_hbm.at[cols, :], w_o.at[2 * core + q], loc_sem.at[5 + q]),
        )

    toks = (fwd_hbm, bwd_hbm, cot_hbm)
    local_t = [pltpu.make_async_copy(toks[t], tok.at[t, core], loc_sem.at[t]) for t in range(3)]
    for q in range(2):
        for copy in local_w(q):
            copy.start()
    for copy in local_t:
        copy.start()

    barrier = pltpu.get_barrier_semaphore()

    def greet(dev):
        pl.semaphore_signal(barrier, inc=1, device_id=dev, device_id_type=MESH)

    greet(peer)
    for core_ in range(2):
        greet(at(chip, core_, orep))
        for rep_ in range(2):
            greet(at(chip + 1, core_, rep_))
            greet(at(chip - 1, core_, rep_))
    for p in (0, 3, 12, 15):
        @pl.when(corner(p))
        def _():
            for other_p in (0, 3, 12, 15):
                if other_p != p:
                    greet(in_plane(other_p))
    is_corner = corner(0) | corner(3) | corner(12) | corner(15)

    @pl.when(jnp.logical_not(is_corner))
    def _():
        pl.semaphore_wait(barrier, 11)

    @pl.when(is_corner)
    def _():
        pl.semaphore_wait(barrier, 14)

    def swap_w(q):
        cols = pl.ds(pl.multiple_of(other * HALF + q * CH, CH), CH)
        return (
            remote(win_hbm.at[:, cols], w_i.at[2 * core + q], wx_send.at[q, 0], wx_recv.at[q, 0], peer),
            remote(wout_hbm.at[cols, :], w_o.at[2 * core + q], wx_send.at[q, 1], wx_recv.at[q, 1], peer),
        )

    swaps = [copy for q in range(2) for copy in swap_w(q)]
    for copy in swaps:
        copy.start()
    swap_t = [
        remote(toks[t], tok.at[t, core], tok_send.at[t], tok_recv.at[t], peer) for t in range(3)
    ]
    for copy in swap_t:
        copy.start()

    def arrived_w(q):
        return (
            pltpu.make_async_remote_copy(
                src_ref=w_i.at[2 * other + q], dst_ref=w_i.at[2 * other + q],
                send_sem=wx_send.at[q, 0], recv_sem=wx_recv.at[q, 0],
                device_id=peer, device_id_type=MESH),
            pltpu.make_async_remote_copy(
                src_ref=w_o.at[2 * other + q], dst_ref=w_o.at[2 * other + q],
                send_sem=wx_send.at[q, 1], recv_sem=wx_recv.at[q, 1],
                device_id=peer, device_id_type=MESH),
        )

    STREAM_F = {0: (None, (0, 768), None), 1: (0, (768, 256), (0, 32)), 2: (12, None, (32, 64)),
                3: (3, None, (96, 32))}
    STREAM_B = {0: (None, 0, 0), 1: (15, 0, 64), 2: (3, 1, 0), 3: (12, 1, 64)}

    def pieces_w(n, s):
        _, rows_i, rows_o = STREAM_F[s]
        out = []
        for a, (ref, rows) in enumerate(((w_i, rows_i), (w_o, rows_o))):
            if rows is not None:
                out.append((a, ref.at[n, pl.ds(*rows)], (rly_i, rly_o)[a], rows[1]))
        return out

    def whole_w(i, n):
        return (
            remote(w_i.at[n], w_i.at[4 + i], xp_send.at[i, 0], xp_recv.at[i, 0], ahead),
            remote(w_o.at[n], w_o.at[4 + i], xp_send.at[i, 1], xp_recv.at[i, 1], ahead),
        )

    first_ahead = at(chip + 1, core, 0)
    sends_f = corner(SRC_F) & (rep == 1)

    def direct_w(i, n):
        _, src, _, _ = pieces_w(n, 0)[0]
        _, dst, _, _ = pieces_w(4 + i, 0)[0]
        return (remote(src, dst, xp_send.at[i, 0], xp_recv.at[i, 0], ahead),
                remote(src, dst, xd_send.at[i], xp_recv.at[i, 0], first_ahead))

    def send_w(i, n):
        @pl.when(jnp.logical_not(corner(SRC_F)))
        def _():
            for copy in whole_w(i, n):
                copy.start()

        @pl.when(sends_f)
        def _():
            for s in (1, 2, 3):
                for a, src, rly, size in pieces_w(n, s):
                    remote(src, rly.at[i, pl.ds(0, size)], xp_send.at[i, a], rf_recv.at[i, a],
                           in_plane(STREAM_F[s][0])).start()
            for copy in direct_w(i, n):
                copy.start()

    def sent_w(i):
        @pl.when(jnp.logical_not(corner(SRC_F)) | sends_f)
        def _():
            for copy in whole_w(i, 4 + i):
                copy.wait_send()

        @pl.when(sends_f)
        def _():
            direct_w(i, 4 + i)[1].wait_send()

    def relays_w(i):
        for s, (via, _, _) in STREAM_F.items():
            if via is not None:
                copies = []
                for a, dst, rly, size in pieces_w(4 + i, s):
                    held = rly.at[i, pl.ds(0, size)]
                    devs = [at((zhi + 1) * 16, core, rep_) for rep_ in range(2)]
                    copies.append((
                        remote(held, held, rf_send.at[i, a, 0], rf_recv.at[i, a], devs[0]),
                        [remote(held, dst, rf_send.at[i, a, rep_], xp_recv.at[i, a], devs[rep_])
                         for rep_ in (1, 0)],
                    ))
                yield via, copies

    def pass_w(i):
        for via, copies in relays_w(i):
            @pl.when(corner(via) & (rep == 1))
            def _():
                for come, gone in copies:
                    come.wait_recv()
                    for go in gone:
                        go.start()

    def passed_w(i):
        for via, copies in relays_w(i):
            @pl.when(corner(via) & (rep == 1))
            def _():
                for come, gone in copies:
                    for go in gone:
                        go.wait_send()

    def parts_g(i):
        q, kind = CHUNK[i], KIND[i]
        if q == 1:
            if kind == 3:
                return [(8, g3.at[2], g3_sem.at[1], core)]
            return [(5 + kind, final.at[2, core, 1], fin_sem.at[2, core, 1], 2 - kind)]
        if kind == 3:
            return [(4 + h, g3.at[h], g3_sem.at[0], core) for h in range(2)]
        return [(2 * kind - 2 + h, lrecv.at[2 - kind, h], l_sem.at[2 - kind], core) for h in range(2)]

    def piece_g(ref, s):
        _, a, row = STREAM_B[s]
        return ref.at[a, pl.ds(row, 64)]

    def send_g(i):
        for slot, dst, sem, core_ in parts_g(i):
            dev = at(chip - 1, core_, rep)

            @pl.when(jnp.logical_not(corner(SRC_B)))
            def _():
                remote(gs.at[slot], dst, xm_send.at[slot], sem, dev).start()

            @pl.when(corner(SRC_B))
            def _():
                for s in (1, 2, 3, 0):
                    via = STREAM_B[s][0]
                    if via is None:
                        remote(piece_g(gs.at[slot], s), piece_g(dst, s), xm_send.at[slot], sem,
                               dev).start()
                    else:
                        remote(piece_g(gs.at[slot], s), rly_b.at[slot], xm_send.at[slot],
                               rb_recv.at[slot], in_plane(via)).start()

    def relays_g(i):
        for slot, dst, sem, core_ in parts_g(i):
            dev = at(zhi * 16 - 1, core_, rep)
            for s, (via, _, _) in STREAM_B.items():
                if via is not None:
                    yield via, (
                        remote(rly_b.at[slot], rly_b.at[slot], rb_send.at[slot], rb_recv.at[slot], dev),
                        remote(rly_b.at[slot], piece_g(dst, s), rb_send.at[slot], sem, dev),
                    )

    def pass_g(i):
        for via, (come, go) in relays_g(i):
            @pl.when(corner(via))
            def _():
                come.wait_recv()
                go.start()

    def passed_g(i):
        for via, (come, go) in relays_g(i):
            @pl.when(corner(via))
            def _():
                go.wait_send()

    def compute(n, lo, hi):
        grad[...] = jnp.zeros_like(grad)

        def block(b, carry):
            wi, wo = w_i[n], w_o[n]
            pre = jnp.dot(tok[0, b], wi, preferred_element_type=F32)
            hid = (0.5 * pre * (1.0 + jnp.tanh(SQ * (pre + 0.044715 * (pre * pre * pre))))).astype(BF16)
            facc[b] += jnp.dot(hid, wo, preferred_element_type=F32)
            pre = jnp.dot(tok[1, b], wi, preferred_element_type=F32)
            hid_grad = inner(tok[2, b], wo, 1, 1)
            square = pre * pre
            t = jnp.tanh(SQ * (pre + 0.044715 * (square * pre)))
            cdf = 0.5 * (1.0 + t)
            slope = cdf + pre * (0.5 * (1.0 - t * t)) * (SQ * (1.0 + 3 * 0.044715 * square))
            hid = (pre * cdf).astype(BF16)
            pre_grad = (hid_grad * slope).astype(BF16)
            iacc[b] += inner(pre_grad, wi, 1, 1)
            grad[0] += inner(pre_grad, tok[1, b], 0, 0)
            grad[1] += inner(hid, tok[2, b], 0, 0)
            return carry

        lax.fori_loop(lo, hi, block, 0)

    def halves(ref, h):
        return ref[:, :, pl.ds(h * 512, 512)]

    for q in range(2):
        for copy in local_w(q):
            copy.wait()
        for copy in arrived_w(q):
            copy.wait_recv()
        send_w(P1C0 + q, 2 + q)
    facc[...] = jnp.zeros_like(facc)
    iacc[...] = jnp.zeros_like(iacc)
    for t in range(3):
        local_t[t].wait()
    for t in range(3):
        remote(toks[t], tok.at[t, other], tok_send.at[t], tok_recv.at[t], peer).wait_recv()

    def own_copy(n, h):
        j, q = n // 2, n % 2
        return remote(own_send.at[n, h], final.at[rep, core, q], own_sem.at[n, h],
                      fin_sem.at[rep, core, q], at(chip, j, h))

    def hand_out(n, h, value):
        mine = (core == n // 2) & (rep == h)

        @pl.when(mine)
        def _():
            keep[n % 2] = value

        @pl.when(jnp.logical_not(mine))
        def _():
            own_send[n, h] = value.astype(BF16)
            own_copy(n, h).start()

    for n in (1, 3):
        compute(n, n // 2, 2)
        for h in range(2):
            hand_out(n, h, halves(grad, h))
    pass_w(P1C0)

    def own_step(j, carry):
        compute(2 * j, j, 2)
        ownfull[j] = grad[...]
        return carry

    lax.fori_loop(0, 2, own_step, 0)
    pass_w(P1C1)

    def merge_own(j):
        remote(lrecv.at[j], lrecv.at[j], z_send.at[0], l_sem.at[j], ahead).wait_recv()
        for h in range(2):
            hand_out(2 * j, h, halves(ownfull.at[j], h) + lrecv[j, h].astype(F32))

    def my_half(ref, h):
        return ref[:, :, pl.ds(pl.multiple_of(h * 512, 512), 512)]

    orep_dev = at(chip, core, orep)

    def swap_z(i):
        return remote(zs.at[i], zr.at[i], z_send.at[i], z_recv.at[i], orep_dev)

    def finish_z(i):
        swap_z(i).wait_recv()
        total = hold[i] + zr[i].astype(F32)
        if KIND[i] == 1:
            hold[i] = total
        else:
            gs[parts_g(i)[0][0]] = total.astype(BF16)
            send_g(i)

    def send_whole(i, more=False):
        for h, (slot, _, _, _) in enumerate(parts_g(i)):
            if more:
                gs[slot] = (halves(p1full, h) + g3[h].astype(F32)).astype(BF16)
            else:
                gs[slot] = halves(grad, h).astype(BF16)
        send_g(i)

    def finish_p1(q):
        if q == 0:
            both = g3.at[pl.ds(0, 2)]
            remote(both, both, z_send.at[0], g3_sem.at[0], ahead).wait_recv()
            send_whole(P1C0, True)
        else:
            remote(g3.at[2], g3.at[2], z_send.at[0], g3_sem.at[1], ahead).wait_recv()
            gs[parts_g(P1C1)[0][0]] = (hold[P1C1] + g3[2].astype(F32)).astype(BF16)
            send_g(P1C1)

    for i in range(6):
        q, kind = CHUNK[i], KIND[i]
        for early in ((), (P3C0,), (P2C0,), (P3C1, P2C1), (), ())[i]:
            pass_w(early)
        if i == 2:
            finish_z(P1C1)
        if i == 4:
            pass_g(P3C0)
            finish_p1(0)
        if i == 5:
            finish_z(P3C1)
            pass_g(P2C0)
        for copy in whole_w(i, 4 + i):
            copy.wait_recv()
        if i == 0:
            send_w(P3C0, 4 + i)
        if i == 1:
            send_w(P2C0, 0)
            send_w(P3C1, 4 + i)
            send_w(P2C1, 1)
        compute(4 + i, 0, 1 if kind == 3 else 2)
        if i == P1C0:
            p1full[...] = grad[...]
        elif q == 0:
            send_whole(i)
        else:
            hold[i] = my_half(grad, rep)
            zs[i] = my_half(grad, orep).astype(BF16)
            swap_z(i).start()

    outs = [
        remote(acc.at[other], orecv.at[a], out_send.at[a], out_recv.at[a], peer)
        for a, acc in enumerate((facc, iacc))
    ]
    for copy in outs:
        copy.start()
    pass_g(P1C0)
    merge_own(0)
    finish_z(P2C1)
    pass_g(P3C1)
    finish_p1(1)
    merge_own(1)
    pass_g(P2C1)
    pass_g(P1C1)

    for a, (acc, out) in enumerate(((facc, fout), (iacc, iout))):
        outs[a].wait_recv()
        out[...] = (acc[core] + orecv[a]).astype(BF16)

    def arrived(slot, core_, q):
        ref = final.at[slot, core_, q]
        remote(ref, ref, z_send.at[0], fin_sem.at[slot, core_, q], ahead).wait_recv()
        return ref[...].astype(F32)

    def finish(q):
        for core_ in (core, other):
            total = keep[q] if core_ is core else arrived(rep, core_, q)
            total = total + arrived(orep, core_, q)
            if q == 1:
                total = total + arrived(2, core_, q)
            at_hid = pl.multiple_of(core_ * HALF + q * CH, CH)
            inout[:, pl.ds(at_hid, CH)] = total[0].T
            downout[pl.ds(at_hid, CH), :] = total[1]

    finish(0)
    finish(1)

    for copy in swaps + swap_t + outs:
        copy.wait_send()
    for i in range(6):
        sent_w(i)
        passed_w(i)
        passed_g(i)
        for slot, _, _, _ in parts_g(i):
            remote(gs.at[slot], gs.at[slot], xm_send.at[slot], g3_sem.at[0], ahead).wait_send()
        if CHUNK[i] == 1:
            swap_z(i).wait_send()
    for n in range(4):
        for h in range(2):
            @pl.when(jnp.logical_not((core == n // 2) & (rep == h)))
            def _():
                own_copy(n, h).wait_send()


def on_device(fwd_in, bwd_in, cotangent, w_in, w_out):
    dma = pltpu.SemaphoreType.DMA
    vmem = pltpu.VMEM
    return pl.pallas_call(
        kernel,
        out_shape=(
            jax.ShapeDtypeStruct((MB, D), BF16),
            jax.ShapeDtypeStruct((MB, D), BF16),
            jax.ShapeDtypeStruct((HID, HID), F32),
            jax.ShapeDtypeStruct((HID, HID), F32),
        ),
        in_specs=[pl.BlockSpec(memory_space=pl.ANY)] * 5,
        out_specs=[pl.BlockSpec(memory_space=pltpu.VMEM)] * 4,
        scratch_shapes=[
            vmem((3, 2, MB, D), BF16),
            vmem((10, D, CH), BF16),
            vmem((10, CH, D), BF16),
            vmem((2, MB, D), F32),
            vmem((2, MB, D), F32),
            vmem((2, MB, D), F32),
            vmem((2, CH, D), F32),
            vmem((4, 2, 2, CH, 512), BF16),
            vmem((9, 2, CH, 512), BF16),
            vmem((6, 2, CH, 512), F32),
            vmem((6, 2, CH, 512), BF16),
            vmem((6, 2, CH, 512), BF16),
            vmem((2, 2, CH, 512), F32),
            vmem((3, 2, 2, 2, CH, 512), BF16),
            vmem((3, 2, CH, 512), BF16),
            vmem((2, CH, D), F32),
            vmem((2, 2, CH, D), F32),
            vmem((2, 2, 2, CH, 512), BF16),
            vmem((6, 256, CH), BF16),
            vmem((6, 64, D), BF16),
            vmem((9, 64, 512), BF16),
            dma((7,)),
            dma((2, 2)),
            dma((2, 2)),
            dma((3,)),
            dma((3,)),
            dma((6, 2)),
            dma((6, 2)),
            dma((6,)),
            dma((6, 2, 2)),
            dma((6, 2)),
            dma((4, 2)),
            dma((3, 2, 2)),
            dma((9,)),
            dma((2,)),
            dma((6,)),
            dma((6,)),
            dma((9,)),
            dma((9,)),
            dma((2,)),
            dma((2,)),
            dma((2,)),
        ],
        compiler_params=pltpu.CompilerParams(
            collective_id=0, has_side_effects=True, vmem_limit_bytes=50 * 2**20
        ),
        cost_estimate=pl.CostEstimate(
            flops=13_153_337_344, bytes_accessed=12 * 2**20, transcendentals=2 * 4 * MB * HID
        ),
    )(fwd_in, bwd_in, cotangent, w_in, w_out)


def solution(mesh):
    in_specs = (
        P(("blk", "rep"), None),
        P(("blk", "rep"), None),
        P(("blk", "rep"), None),
        P(None, "blk"),
        P("blk", None),
    )
    out_specs = (P(("blk", "rep"), None), P(("blk", "rep"), None), P("rep", "blk"), P("blk", "rep"))
    return jax.shard_map(
        on_device, mesh=mesh, in_specs=in_specs, out_specs=out_specs, check_vma=False
    )
```

```python
import jax
import jax.numpy as jnp
from jax import lax
from jax.experimental import pallas as pl
from jax.experimental.pallas import tpu as pltpu
from jax.sharding import PartitionSpec as P

MESH = pl.DeviceIdType.MESH
MB, D, HID, CH = 448, 1024, 512, 128
HALF = HID // 2
F32, BF16 = jnp.float32, jnp.bfloat16
SQ = 0.7978845608028654

P1C0, P1C1, P3C0, P2C0, P3C1, P2C1 = range(6)
KIND, CHUNK = (1, 1, 3, 2, 3, 2), (0, 1, 0, 0, 1, 1)


def inner(left, right, left_dim, right_dim):
    return lax.dot_general(
        left, right, (((left_dim,), (right_dim,)), ((), ())), preferred_element_type=F32
    )


def kernel(
    fwd_hbm, bwd_hbm, cot_hbm, win_hbm, wout_hbm,
    fout, iout, inout, downout,
    tok, w_i, w_o, facc, iacc, orecv, grad, own_send, gs, hold, zs, zr, keep, final, g3,
    p1full, ownfull, lrecv,
    rly_i, rly_o, rly_b,
    loc_sem, wx_send, wx_recv, tok_send, tok_recv,
    xp_send, xp_recv, xd_send, rf_send, rf_recv,
    own_sem, fin_sem, xm_send, g3_sem, z_send, z_recv, rb_send, rb_recv, out_send, out_recv, l_sem,
):
    blk, rep = lax.axis_index("blk"), lax.axis_index("rep")
    core = lax.rem(blk, 2)
    chip = lax.div(blk, 2)
    pos = lax.rem(chip, 16)
    zhi = lax.div(chip, 16)
    other, orep = 1 - core, 1 - rep

    def at(chip_, core_, rep_):
        return (lax.rem(chip_ + 64, 64) * 2 + core_, rep_)

    def corner(p):
        return pos == p

    def in_plane(p, core_=core):
        return at(zhi * 16 + p, core_, rep)

    def remote(src, dst, ssem, rsem, dev):
        return pltpu.make_async_remote_copy(
            src_ref=src, dst_ref=dst, send_sem=ssem, recv_sem=rsem,
            device_id=dev, device_id_type=MESH,
        )

    peer = at(chip, other, rep)
    ahead = at(chip + 1, core, rep)
    SRC_F, SRC_B = 15, 0

    def local_w(q):
        cols = pl.ds(pl.multiple_of(core * HALF + q * CH, CH), CH)
        return (
            pltpu.make_async_copy(win_hbm.at[:, cols], w_i.at[2 * core + q], loc_sem.at[3 + q]),
            pltpu.make_async_copy(wout_hbm.at[cols, :], w_o.at[2 * core + q], loc_sem.at[5 + q]),
        )

    toks = (fwd_hbm, bwd_hbm, cot_hbm)
    local_t = [pltpu.make_async_copy(toks[t], tok.at[t, core], loc_sem.at[t]) for t in range(3)]
    for q in range(2):
        for copy in local_w(q):
            copy.start()
    for copy in local_t:
        copy.start()

    barrier = pltpu.get_barrier_semaphore()

    def greet(dev):
        pl.semaphore_signal(barrier, inc=1, device_id=dev, device_id_type=MESH)

    greet(peer)
    for core_ in range(2):
        greet(at(chip, core_, orep))
        for rep_ in range(2):
            greet(at(chip + 1, core_, rep_))
            greet(at(chip - 1, core_, rep_))
    for p in (0, 3, 12, 15):
        @pl.when(corner(p))
        def _():
            for other_p in (0, 3, 12, 15):
                if other_p != p:
                    greet(in_plane(other_p))
    is_corner = corner(0) | corner(3) | corner(12) | corner(15)

    @pl.when(jnp.logical_not(is_corner))
    def _():
        pl.semaphore_wait(barrier, 11)

    @pl.when(is_corner)
    def _():
        pl.semaphore_wait(barrier, 14)

    def swap_w(q):
        cols = pl.ds(pl.multiple_of(other * HALF + q * CH, CH), CH)
        return (
            remote(win_hbm.at[:, cols], w_i.at[2 * core + q], wx_send.at[q, 0], wx_recv.at[q, 0], peer),
            remote(wout_hbm.at[cols, :], w_o.at[2 * core + q], wx_send.at[q, 1], wx_recv.at[q, 1], peer),
        )

    swaps = [copy for q in range(2) for copy in swap_w(q)]
    for copy in swaps:
        copy.start()
    swap_t = [
        remote(toks[t], tok.at[t, core], tok_send.at[t], tok_recv.at[t], peer) for t in range(3)
    ]
    for copy in swap_t:
        copy.start()

    def arrived_w(q):
        return (
            pltpu.make_async_remote_copy(
                src_ref=w_i.at[2 * other + q], dst_ref=w_i.at[2 * other + q],
                send_sem=wx_send.at[q, 0], recv_sem=wx_recv.at[q, 0],
                device_id=peer, device_id_type=MESH),
            pltpu.make_async_remote_copy(
                src_ref=w_o.at[2 * other + q], dst_ref=w_o.at[2 * other + q],
                send_sem=wx_send.at[q, 1], recv_sem=wx_recv.at[q, 1],
                device_id=peer, device_id_type=MESH),
        )

    STREAM_F = {0: (None, (0, 512), None), 1: (0, (512, 512), (0, 32)), 2: (12, None, (32, 48)),
                3: (3, None, (80, 48))}
    STREAM_B = {0: (None, 0, 0, 64), 1: (15, 0, 64, 64), 2: (3, 1, 0, 64), 3: (12, 1, 64, 64)}

    def pieces_w(n, s):
        _, rows_i, rows_o = STREAM_F[s]
        out = []
        for a, (ref, rows) in enumerate(((w_i, rows_i), (w_o, rows_o))):
            if rows is not None:
                out.append((a, ref.at[n, pl.ds(*rows)], (rly_i, rly_o)[a], rows[1]))
        return out

    def whole_w(i, n):
        return (
            remote(w_i.at[n], w_i.at[4 + i], xp_send.at[i, 0], xp_recv.at[i, 0], ahead),
            remote(w_o.at[n], w_o.at[4 + i], xp_send.at[i, 1], xp_recv.at[i, 1], ahead),
        )

    first_ahead = at(chip + 1, core, 0)
    sends_f = corner(SRC_F) & (rep == 1)

    def direct_w(i, n):
        _, src, _, _ = pieces_w(n, 0)[0]
        _, dst, _, _ = pieces_w(4 + i, 0)[0]
        return (remote(src, dst, xp_send.at[i, 0], xp_recv.at[i, 0], ahead),
                remote(src, dst, xd_send.at[i], xp_recv.at[i, 0], first_ahead))

    def send_w(i, n):
        @pl.when(jnp.logical_not(corner(SRC_F)))
        def _():
            for copy in whole_w(i, n):
                copy.start()

        @pl.when(sends_f)
        def _():
            for s in (1, 2, 3):
                for a, src, rly, size in pieces_w(n, s):
                    remote(src, rly.at[i, pl.ds(0, size)], xp_send.at[i, a], rf_recv.at[i, a],
                           in_plane(STREAM_F[s][0])).start()
            for copy in direct_w(i, n):
                copy.start()

    def sent_w(i):
        @pl.when(jnp.logical_not(corner(SRC_F)) | sends_f)
        def _():
            for copy in whole_w(i, 4 + i):
                copy.wait_send()

        @pl.when(sends_f)
        def _():
            direct_w(i, 4 + i)[1].wait_send()

    def relays_w(i):
        for s, (via, _, _) in STREAM_F.items():
            if via is not None:
                copies = []
                for a, dst, rly, size in pieces_w(4 + i, s):
                    held = rly.at[i, pl.ds(0, size)]
                    devs = [at((zhi + 1) * 16, core, rep_) for rep_ in range(2)]
                    copies.append((
                        remote(held, held, rf_send.at[i, a, 0], rf_recv.at[i, a], devs[0]),
                        [remote(held, dst, rf_send.at[i, a, rep_], xp_recv.at[i, a], devs[rep_])
                         for rep_ in (1, 0)],
                    ))
                yield via, copies

    def pass_w(i):
        for via, copies in relays_w(i):
            @pl.when(corner(via) & (rep == 1))
            def _():
                for come, gone in copies:
                    come.wait_recv()
                    for go in gone:
                        go.start()

    def passed_w(i):
        for via, copies in relays_w(i):
            @pl.when(corner(via) & (rep == 1))
            def _():
                for come, gone in copies:
                    for go in gone:
                        go.wait_send()

    def parts_g(i):
        q, kind = CHUNK[i], KIND[i]
        if q == 1:
            if kind == 3:
                return [(8, g3.at[2], g3_sem.at[1], core)]
            return [(5 + kind, final.at[2, core, 1], fin_sem.at[2, core, 1], 2 - kind)]
        if kind == 3:
            return [(4 + h, g3.at[h], g3_sem.at[0], core) for h in range(2)]
        return [(2 * kind - 2 + h, lrecv.at[2 - kind, h], l_sem.at[2 - kind], core) for h in range(2)]

    def piece_g(ref, s):
        _, a, row, size = STREAM_B[s]
        return ref.at[a, pl.ds(row, size)]

    def held_g(slot, s):
        return rly_b.at[slot, pl.ds(0, STREAM_B[s][3])]

    def send_g(i):
        for slot, dst, sem, core_ in parts_g(i):
            dev = at(chip - 1, core_, rep)

            @pl.when(jnp.logical_not(corner(SRC_B)))
            def _():
                remote(gs.at[slot], dst, xm_send.at[slot], sem, dev).start()

            @pl.when(corner(SRC_B))
            def _():
                for s in (1, 2, 3, 0):
                    via = STREAM_B[s][0]
                    if via is None:
                        remote(piece_g(gs.at[slot], s), piece_g(dst, s), xm_send.at[slot], sem,
                               dev).start()
                    else:
                        remote(piece_g(gs.at[slot], s), held_g(slot, s), xm_send.at[slot],
                               rb_recv.at[slot], in_plane(via)).start()

    def relays_g(i):
        for slot, dst, sem, core_ in parts_g(i):
            dev = at(zhi * 16 - 1, core_, rep)
            for s, (via, _, _, _) in STREAM_B.items():
                if via is not None:
                    yield via, (
                        remote(held_g(slot, s), held_g(slot, s), rb_send.at[slot], rb_recv.at[slot], dev),
                        remote(held_g(slot, s), piece_g(dst, s), rb_send.at[slot], sem, dev),
                    )

    def pass_g(i):
        for via, (come, go) in relays_g(i):
            @pl.when(corner(via))
            def _():
                come.wait_recv()
                go.start()

    def passed_g(i):
        for via, (come, go) in relays_g(i):
            @pl.when(corner(via))
            def _():
                go.wait_send()

    def compute(n, lo, hi):
        grad[...] = jnp.zeros_like(grad)

        def block(b, carry):
            wi, wo = w_i[n], w_o[n]
            pre = jnp.dot(tok[0, b], wi, preferred_element_type=F32)
            hid = (0.5 * pre * (1.0 + jnp.tanh(SQ * (pre + 0.044715 * (pre * pre * pre))))).astype(BF16)
            facc[b] += jnp.dot(hid, wo, preferred_element_type=F32)
            pre = jnp.dot(tok[1, b], wi, preferred_element_type=F32)
            hid_grad = inner(tok[2, b], wo, 1, 1)
            square = pre * pre
            t = jnp.tanh(SQ * (pre + 0.044715 * (square * pre)))
            cdf = 0.5 * (1.0 + t)
            slope = cdf + pre * (0.5 * (1.0 - t * t)) * (SQ * (1.0 + 3 * 0.044715 * square))
            hid = (pre * cdf).astype(BF16)
            pre_grad = (hid_grad * slope).astype(BF16)
            iacc[b] += inner(pre_grad, wi, 1, 1)
            grad[0] += inner(pre_grad, tok[1, b], 0, 0)
            grad[1] += inner(hid, tok[2, b], 0, 0)
            return carry

        lax.fori_loop(lo, hi, block, 0)

    def halves(ref, h):
        return ref[:, :, pl.ds(h * 512, 512)]

    for q in range(2):
        for copy in local_w(q):
            copy.wait()
        for copy in arrived_w(q):
            copy.wait_recv()
        send_w(P1C0 + q, 2 + q)
    facc[...] = jnp.zeros_like(facc)
    iacc[...] = jnp.zeros_like(iacc)
    for t in range(3):
        local_t[t].wait()
    for t in range(3):
        remote(toks[t], tok.at[t, other], tok_send.at[t], tok_recv.at[t], peer).wait_recv()

    def own_copy(n, h):
        j, q = n // 2, n % 2
        return remote(own_send.at[n, h], final.at[rep, core, q], own_sem.at[n, h],
                      fin_sem.at[rep, core, q], at(chip, j, h))

    def hand_out(n, h, value):
        mine = (core == n // 2) & (rep == h)

        @pl.when(mine)
        def _():
            keep[n % 2] = value

        @pl.when(jnp.logical_not(mine))
        def _():
            own_send[n, h] = value.astype(BF16)
            own_copy(n, h).start()

    for n in (1, 3):
        compute(n, n // 2, 2)
        for h in range(2):
            hand_out(n, h, halves(grad, h))
    pass_w(P1C0)

    def own_step(j, carry):
        compute(2 * j, j, 2)
        ownfull[j] = grad[...]
        return carry

    lax.fori_loop(0, 2, own_step, 0)
    pass_w(P1C1)

    def merge_own(j):
        remote(lrecv.at[j], lrecv.at[j], z_send.at[0], l_sem.at[j], ahead).wait_recv()
        for h in range(2):
            hand_out(2 * j, h, halves(ownfull.at[j], h) + lrecv[j, h].astype(F32))

    def my_half(ref, h):
        return ref[:, :, pl.ds(pl.multiple_of(h * 512, 512), 512)]

    orep_dev = at(chip, core, orep)

    def swap_z(i):
        return remote(zs.at[i], zr.at[i], z_send.at[i], z_recv.at[i], orep_dev)

    def finish_z(i):
        swap_z(i).wait_recv()
        total = hold[i] + zr[i].astype(F32)
        if KIND[i] == 1:
            hold[i] = total
        else:
            gs[parts_g(i)[0][0]] = total.astype(BF16)
            send_g(i)

    def send_whole(i, more=False):
        for h, (slot, _, _, _) in enumerate(parts_g(i)):
            if more:
                gs[slot] = (halves(p1full, h) + g3[h].astype(F32)).astype(BF16)
            else:
                gs[slot] = halves(grad, h).astype(BF16)
        send_g(i)

    def finish_p1(q):
        if q == 0:
            both = g3.at[pl.ds(0, 2)]
            remote(both, both, z_send.at[0], g3_sem.at[0], ahead).wait_recv()
            send_whole(P1C0, True)
        else:
            remote(g3.at[2], g3.at[2], z_send.at[0], g3_sem.at[1], ahead).wait_recv()
            gs[parts_g(P1C1)[0][0]] = (hold[P1C1] + g3[2].astype(F32)).astype(BF16)
            send_g(P1C1)

    for i in range(6):
        q, kind = CHUNK[i], KIND[i]
        for early in ((), (P3C0,), (P2C0,), (P3C1, P2C1), (), ())[i]:
            pass_w(early)
        if i == 2:
            finish_z(P1C1)
        if i == 4:
            pass_g(P3C0)
            finish_p1(0)
        if i == 5:
            finish_z(P3C1)
            pass_g(P2C0)
        for copy in whole_w(i, 4 + i):
            copy.wait_recv()
        if i == 0:
            send_w(P3C0, 4 + i)
        if i == 1:
            send_w(P2C0, 0)
            send_w(P3C1, 4 + i)
            send_w(P2C1, 1)
        compute(4 + i, 0, 1 if kind == 3 else 2)
        if i == P1C0:
            p1full[...] = grad[...]
        elif q == 0:
            send_whole(i)
        else:
            hold[i] = my_half(grad, rep)
            zs[i] = my_half(grad, orep).astype(BF16)
            swap_z(i).start()

    outs = [
        remote(acc.at[other], orecv.at[a], out_send.at[a], out_recv.at[a], peer)
        for a, acc in enumerate((facc, iacc))
    ]
    for copy in outs:
        copy.start()
    pass_g(P1C0)
    merge_own(0)
    finish_z(P2C1)
    pass_g(P3C1)
    finish_p1(1)
    merge_own(1)
    pass_g(P2C1)
    pass_g(P1C1)

    for a, (acc, out) in enumerate(((facc, fout), (iacc, iout))):
        outs[a].wait_recv()
        out[...] = (acc[core] + orecv[a]).astype(BF16)

    def arrived(slot, core_, q):
        ref = final.at[slot, core_, q]
        remote(ref, ref, z_send.at[0], fin_sem.at[slot, core_, q], ahead).wait_recv()
        return ref[...].astype(F32)

    def finish(q):
        for core_ in (core, other):
            total = keep[q] if core_ is core else arrived(rep, core_, q)
            total = total + arrived(orep, core_, q)
            if q == 1:
                total = total + arrived(2, core_, q)
            at_hid = pl.multiple_of(core_ * HALF + q * CH, CH)
            inout[:, pl.ds(at_hid, CH)] = total[0].T
            downout[pl.ds(at_hid, CH), :] = total[1]

    finish(0)
    finish(1)

    for copy in swaps + swap_t + outs:
        copy.wait_send()
    for i in range(6):
        sent_w(i)
        passed_w(i)
        passed_g(i)
        for slot, _, _, _ in parts_g(i):
            remote(gs.at[slot], gs.at[slot], xm_send.at[slot], g3_sem.at[0], ahead).wait_send()
        if CHUNK[i] == 1:
            swap_z(i).wait_send()
    for n in range(4):
        for h in range(2):
            @pl.when(jnp.logical_not((core == n // 2) & (rep == h)))
            def _():
                own_copy(n, h).wait_send()


def hand_on(a, b, c, d, ao, bo, co, do):
    for src, dst in ((a, ao), (b, bo), (c, co), (d, do)):
        dst[...] = src[...]


def on_device(fwd_in, bwd_in, cotangent, w_in, w_out):
    dma = pltpu.SemaphoreType.DMA
    vmem = pltpu.VMEM
    results = pl.pallas_call(
        kernel,
        out_shape=(
            jax.ShapeDtypeStruct((MB, D), BF16),
            jax.ShapeDtypeStruct((MB, D), BF16),
            jax.ShapeDtypeStruct((HID, HID), F32),
            jax.ShapeDtypeStruct((HID, HID), F32),
        ),
        in_specs=[pl.BlockSpec(memory_space=pl.ANY)] * 5,
        out_specs=[pl.BlockSpec(memory_space=pltpu.VMEM)] * 4,
        scratch_shapes=[
            vmem((3, 2, MB, D), BF16),
            vmem((10, D, CH), BF16),
            vmem((10, CH, D), BF16),
            vmem((2, MB, D), F32),
            vmem((2, MB, D), F32),
            vmem((2, MB, D), F32),
            vmem((2, CH, D), F32),
            vmem((4, 2, 2, CH, 512), BF16),
            vmem((9, 2, CH, 512), BF16),
            vmem((6, 2, CH, 512), F32),
            vmem((6, 2, CH, 512), BF16),
            vmem((6, 2, CH, 512), BF16),
            vmem((2, 2, CH, 512), F32),
            vmem((3, 2, 2, 2, CH, 512), BF16),
            vmem((3, 2, CH, 512), BF16),
            vmem((2, CH, D), F32),
            vmem((2, 2, CH, D), F32),
            vmem((2, 2, 2, CH, 512), BF16),
            vmem((6, 512, CH), BF16),
            vmem((6, 64, D), BF16),
            vmem((9, 96, 512), BF16),
            dma((7,)),
            dma((2, 2)),
            dma((2, 2)),
            dma((3,)),
            dma((3,)),
            dma((6, 2)),
            dma((6, 2)),
            dma((6,)),
            dma((6, 2, 2)),
            dma((6, 2)),
            dma((4, 2)),
            dma((3, 2, 2)),
            dma((9,)),
            dma((2,)),
            dma((6,)),
            dma((6,)),
            dma((9,)),
            dma((9,)),
            dma((2,)),
            dma((2,)),
            dma((2,)),
        ],
        compiler_params=pltpu.CompilerParams(
            collective_id=0, has_side_effects=True, vmem_limit_bytes=60 * 2**20
        ),
        cost_estimate=pl.CostEstimate(
            flops=13_153_337_344, bytes_accessed=12 * 2**20, transcendentals=2 * 4 * MB * HID
        ),
    )(fwd_in, bwd_in, cotangent, w_in, w_out)
    steps = 4
    blocks = [
        pl.BlockSpec((r.shape[0] // steps, r.shape[1]), lambda step: (step, 0)) for r in results
    ]
    return pl.pallas_call(
        hand_on,
        grid=(steps,),
        out_shape=tuple(jax.ShapeDtypeStruct(r.shape, r.dtype) for r in results),
        in_specs=blocks,
        out_specs=blocks,
        compiler_params=pltpu.CompilerParams(vmem_limit_bytes=60 * 2**20),
    )(*results)


def solution(mesh):
    in_specs = (
        P(("blk", "rep"), None),
        P(("blk", "rep"), None),
        P(("blk", "rep"), None),
        P(None, "blk"),
        P("blk", None),
    )
    out_specs = (P(("blk", "rep"), None), P(("blk", "rep"), None), P("rep", "blk"), P("blk", "rep"))
    return jax.shard_map(
        on_device, mesh=mesh, in_specs=in_specs, out_specs=out_specs, check_vma=False
    )
```

```python
import jax
import jax.numpy as jnp
from jax import lax
from jax.experimental import pallas as pl
from jax.experimental.pallas import tpu as pltpu
from jax.sharding import PartitionSpec as P

MESH = pl.DeviceIdType.MESH
MB, D, HID, CH = 448, 1024, 512, 128
HALF = HID // 2
F32, BF16 = jnp.float32, jnp.bfloat16
SQ = 0.7978845608028654

P1C0, P1C1, P3C0, P2C0, P3C1, P2C1 = range(6)
KIND, CHUNK = (1, 1, 3, 2, 3, 2), (0, 1, 0, 0, 1, 1)


def inner(left, right, left_dim, right_dim):
    return lax.dot_general(
        left, right, (((left_dim,), (right_dim,)), ((), ())), preferred_element_type=F32
    )


def kernel(
    fwd_hbm, bwd_hbm, cot_hbm, win_hbm, wout_hbm,
    fout, iout, inout, downout,
    tok, w_i, w_o, facc, iacc, orecv, grad, own_send, gs, hold, zs, zr, keep, final, g3,
    p1full, ownfull, lrecv,
    rly_i, rly_o, rly_b,
    loc_sem, wx_send, wx_recv, tok_send, tok_recv,
    xp_send, xp_recv, xd_send, rf_send, rf_recv,
    own_sem, fin_sem, xm_send, g3_sem, z_send, z_recv, rb_send, rb_recv, out_send, out_recv, l_sem,
):
    blk, rep = lax.axis_index("blk"), lax.axis_index("rep")
    core = lax.rem(blk, 2)
    chip = lax.div(blk, 2)
    pos = lax.rem(chip, 16)
    zhi = lax.div(chip, 16)
    other, orep = 1 - core, 1 - rep

    def at(chip_, core_, rep_):
        return (lax.rem(chip_ + 64, 64) * 2 + core_, rep_)

    def corner(p):
        return pos == p

    def in_plane(p, core_=core):
        return at(zhi * 16 + p, core_, rep)

    def remote(src, dst, ssem, rsem, dev):
        return pltpu.make_async_remote_copy(
            src_ref=src, dst_ref=dst, send_sem=ssem, recv_sem=rsem,
            device_id=dev, device_id_type=MESH,
        )

    peer = at(chip, other, rep)
    ahead = at(chip + 1, core, rep)
    SRC_F, SRC_B = 15, 0

    def local_w(q):
        cols = pl.ds(pl.multiple_of(core * HALF + q * CH, CH), CH)
        return (
            pltpu.make_async_copy(win_hbm.at[:, cols], w_i.at[2 * core + q], loc_sem.at[3 + q]),
            pltpu.make_async_copy(wout_hbm.at[cols, :], w_o.at[2 * core + q], loc_sem.at[5 + q]),
        )

    toks = (fwd_hbm, bwd_hbm, cot_hbm)
    local_t = [pltpu.make_async_copy(toks[t], tok.at[t, core], loc_sem.at[t]) for t in range(3)]
    for q in range(2):
        for copy in local_w(q):
            copy.start()
    for copy in local_t:
        copy.start()

    barrier = pltpu.get_barrier_semaphore()

    def greet(dev):
        pl.semaphore_signal(barrier, inc=1, device_id=dev, device_id_type=MESH)

    greet(peer)
    for core_ in range(2):
        greet(at(chip, core_, orep))
        for rep_ in range(2):
            greet(at(chip + 1, core_, rep_))
            greet(at(chip - 1, core_, rep_))
    for p in (0, 3, 12, 15):
        @pl.when(corner(p))
        def _():
            for other_p in (0, 3, 12, 15):
                if other_p != p:
                    greet(in_plane(other_p))
    is_corner = corner(0) | corner(3) | corner(12) | corner(15)

    @pl.when(jnp.logical_not(is_corner))
    def _():
        pl.semaphore_wait(barrier, 11)

    @pl.when(is_corner)
    def _():
        pl.semaphore_wait(barrier, 14)

    def swap_w(q):
        cols = pl.ds(pl.multiple_of(other * HALF + q * CH, CH), CH)
        return (
            remote(win_hbm.at[:, cols], w_i.at[2 * core + q], wx_send.at[q, 0], wx_recv.at[q, 0], peer),
            remote(wout_hbm.at[cols, :], w_o.at[2 * core + q], wx_send.at[q, 1], wx_recv.at[q, 1], peer),
        )

    swaps = [copy for q in range(2) for copy in swap_w(q)]
    for copy in swaps:
        copy.start()
    swap_t = [
        remote(toks[t], tok.at[t, core], tok_send.at[t], tok_recv.at[t], peer) for t in range(3)
    ]
    for copy in swap_t:
        copy.start()

    def arrived_w(q):
        return (
            pltpu.make_async_remote_copy(
                src_ref=w_i.at[2 * other + q], dst_ref=w_i.at[2 * other + q],
                send_sem=wx_send.at[q, 0], recv_sem=wx_recv.at[q, 0],
                device_id=peer, device_id_type=MESH),
            pltpu.make_async_remote_copy(
                src_ref=w_o.at[2 * other + q], dst_ref=w_o.at[2 * other + q],
                send_sem=wx_send.at[q, 1], recv_sem=wx_recv.at[q, 1],
                device_id=peer, device_id_type=MESH),
        )

    STREAM_F = {0: (None, (0, 512), None), 1: (0, (512, 512), (0, 32)), 2: (12, None, (32, 48)),
                3: (3, None, (80, 48))}
    STREAM_B = {0: (None, 0, 0, 64), 1: (15, 0, 64, 64), 2: (3, 1, 0, 64), 3: (12, 1, 64, 64)}

    def pieces_w(n, s):
        _, rows_i, rows_o = STREAM_F[s]
        out = []
        for a, (ref, rows) in enumerate(((w_i, rows_i), (w_o, rows_o))):
            if rows is not None:
                out.append((a, ref.at[n, pl.ds(*rows)], (rly_i, rly_o)[a], rows[1]))
        return out

    def whole_w(i, n):
        return (
            remote(w_i.at[n], w_i.at[4 + i], xp_send.at[i, 0], xp_recv.at[i, 0], ahead),
            remote(w_o.at[n], w_o.at[4 + i], xp_send.at[i, 1], xp_recv.at[i, 1], ahead),
        )

    first_ahead = at(chip + 1, core, 0)
    sends_f = corner(SRC_F) & (rep == 1)

    def direct_w(i, n):
        _, src, _, _ = pieces_w(n, 0)[0]
        _, dst, _, _ = pieces_w(4 + i, 0)[0]
        return (remote(src, dst, xp_send.at[i, 0], xp_recv.at[i, 0], ahead),
                remote(src, dst, xd_send.at[i], xp_recv.at[i, 0], first_ahead))

    def send_w(i, n):
        @pl.when(jnp.logical_not(corner(SRC_F)))
        def _():
            for copy in whole_w(i, n):
                copy.start()

        @pl.when(sends_f)
        def _():
            for s in (1, 2, 3):
                for a, src, rly, size in pieces_w(n, s):
                    remote(src, rly.at[i, pl.ds(0, size)], xp_send.at[i, a], rf_recv.at[i, a],
                           in_plane(STREAM_F[s][0])).start()
            for copy in direct_w(i, n):
                copy.start()

    def sent_w(i):
        @pl.when(jnp.logical_not(corner(SRC_F)) | sends_f)
        def _():
            for copy in whole_w(i, 4 + i):
                copy.wait_send()

        @pl.when(sends_f)
        def _():
            direct_w(i, 4 + i)[1].wait_send()

    def relays_w(i):
        for s, (via, _, _) in STREAM_F.items():
            if via is not None:
                copies = []
                for a, dst, rly, size in pieces_w(4 + i, s):
                    held = rly.at[i, pl.ds(0, size)]
                    devs = [at((zhi + 1) * 16, core, rep_) for rep_ in range(2)]
                    copies.append((
                        remote(held, held, rf_send.at[i, a, 0], rf_recv.at[i, a], devs[0]),
                        [remote(held, dst, rf_send.at[i, a, rep_], xp_recv.at[i, a], devs[rep_])
                         for rep_ in (1, 0)],
                    ))
                yield via, copies

    def pass_w(i):
        for via, copies in relays_w(i):
            @pl.when(corner(via) & (rep == 1))
            def _():
                for come, gone in copies:
                    come.wait_recv()
                    for go in gone:
                        go.start()

    def passed_w(i):
        for via, copies in relays_w(i):
            @pl.when(corner(via) & (rep == 1))
            def _():
                for come, gone in copies:
                    for go in gone:
                        go.wait_send()

    def parts_g(i):
        q, kind = CHUNK[i], KIND[i]
        if q == 1:
            if kind == 3:
                return [(8, g3.at[2], g3_sem.at[1], core)]
            return [(5 + kind, final.at[2, core, 1], fin_sem.at[2, core, 1], 2 - kind)]
        if kind == 3:
            return [(4 + h, g3.at[h], g3_sem.at[0], core) for h in range(2)]
        return [(2 * kind - 2 + h, lrecv.at[2 - kind, h], l_sem.at[2 - kind], core) for h in range(2)]

    def piece_g(ref, s):
        _, a, row, size = STREAM_B[s]
        return ref.at[a, pl.ds(row, size)]

    def held_g(slot, s):
        return rly_b.at[slot, pl.ds(0, STREAM_B[s][3])]

    def send_g(i):
        for slot, dst, sem, core_ in parts_g(i):
            dev = at(chip - 1, core_, rep)

            @pl.when(jnp.logical_not(corner(SRC_B)))
            def _():
                remote(gs.at[slot], dst, xm_send.at[slot], sem, dev).start()

            @pl.when(corner(SRC_B))
            def _():
                for s in (1, 2, 3, 0):
                    via = STREAM_B[s][0]
                    if via is None:
                        remote(piece_g(gs.at[slot], s), piece_g(dst, s), xm_send.at[slot], sem,
                               dev).start()
                    else:
                        remote(piece_g(gs.at[slot], s), held_g(slot, s), xm_send.at[slot],
                               rb_recv.at[slot], in_plane(via)).start()

    def relays_g(i):
        for slot, dst, sem, core_ in parts_g(i):
            dev = at(zhi * 16 - 1, core_, rep)
            for s, (via, _, _, _) in STREAM_B.items():
                if via is not None:
                    yield via, (
                        remote(held_g(slot, s), held_g(slot, s), rb_send.at[slot], rb_recv.at[slot], dev),
                        remote(held_g(slot, s), piece_g(dst, s), rb_send.at[slot], sem, dev),
                    )

    def pass_g(i):
        for via, (come, go) in relays_g(i):
            @pl.when(corner(via))
            def _():
                come.wait_recv()
                go.start()

    def passed_g(i):
        for via, (come, go) in relays_g(i):
            @pl.when(corner(via))
            def _():
                go.wait_send()

    def compute(n, lo, hi):
        grad[...] = jnp.zeros_like(grad)

        def block(b, carry):
            wi, wo = w_i[n], w_o[n]
            pre = jnp.dot(tok[0, b], wi, preferred_element_type=F32)
            hid = (0.5 * pre * (1.0 + jnp.tanh(SQ * (pre + 0.044715 * (pre * pre * pre))))).astype(BF16)
            facc[b] += jnp.dot(hid, wo, preferred_element_type=F32)
            pre = jnp.dot(tok[1, b], wi, preferred_element_type=F32)
            hid_grad = inner(tok[2, b], wo, 1, 1)
            square = pre * pre
            t = jnp.tanh(SQ * (pre + 0.044715 * (square * pre)))
            cdf = 0.5 * (1.0 + t)
            slope = cdf + pre * (0.5 * (1.0 - t * t)) * (SQ * (1.0 + 3 * 0.044715 * square))
            hid = (pre * cdf).astype(BF16)
            pre_grad = (hid_grad * slope).astype(BF16)
            iacc[b] += inner(pre_grad, wi, 1, 1)
            grad[0] += inner(pre_grad, tok[1, b], 0, 0)
            grad[1] += inner(hid, tok[2, b], 0, 0)
            return carry

        lax.fori_loop(lo, hi, block, 0)

    def halves(ref, h):
        return ref[:, :, pl.ds(h * 512, 512)]

    for q in range(2):
        for copy in local_w(q):
            copy.wait()
        for copy in arrived_w(q):
            copy.wait_recv()
        send_w(P1C0 + q, 2 + q)
    facc[...] = jnp.zeros_like(facc)
    iacc[...] = jnp.zeros_like(iacc)
    for t in range(3):
        local_t[t].wait()
    for t in range(3):
        remote(toks[t], tok.at[t, other], tok_send.at[t], tok_recv.at[t], peer).wait_recv()

    def own_copy(n, h):
        j, q = n // 2, n % 2
        return remote(own_send.at[n, h], final.at[rep, core, q], own_sem.at[n, h],
                      fin_sem.at[rep, core, q], at(chip, j, h))

    def hand_out(n, h, value):
        mine = (core == n // 2) & (rep == h)

        @pl.when(mine)
        def _():
            keep[n % 2] = value

        @pl.when(jnp.logical_not(mine))
        def _():
            own_send[n, h] = value.astype(BF16)
            own_copy(n, h).start()

    for n in (1, 3):
        compute(n, n // 2, 2)
        for h in range(2):
            hand_out(n, h, halves(grad, h))
        pass_w(P1C0 if n == 1 else P1C1)

    def own_step(j, carry):
        compute(2 * j, j, 2)
        ownfull[j] = grad[...]
        return carry

    lax.fori_loop(0, 2, own_step, 0)

    def merge_own(j):
        remote(lrecv.at[j], lrecv.at[j], z_send.at[0], l_sem.at[j], ahead).wait_recv()
        for h in range(2):
            hand_out(2 * j, h, halves(ownfull.at[j], h) + lrecv[j, h].astype(F32))

    def my_half(ref, h):
        return ref[:, :, pl.ds(pl.multiple_of(h * 512, 512), 512)]

    orep_dev = at(chip, core, orep)

    def swap_z(i):
        return remote(zs.at[i], zr.at[i], z_send.at[i], z_recv.at[i], orep_dev)

    def finish_z(i):
        swap_z(i).wait_recv()
        total = hold[i] + zr[i].astype(F32)
        if KIND[i] == 1:
            hold[i] = total
        else:
            gs[parts_g(i)[0][0]] = total.astype(BF16)
            send_g(i)

    def send_whole(i, more=False):
        for h, (slot, _, _, _) in enumerate(parts_g(i)):
            if more:
                gs[slot] = (halves(p1full, h) + g3[h].astype(F32)).astype(BF16)
            else:
                gs[slot] = halves(grad, h).astype(BF16)
        send_g(i)

    def finish_p1(q):
        if q == 0:
            both = g3.at[pl.ds(0, 2)]
            remote(both, both, z_send.at[0], g3_sem.at[0], ahead).wait_recv()
            send_whole(P1C0, True)
        else:
            remote(g3.at[2], g3.at[2], z_send.at[0], g3_sem.at[1], ahead).wait_recv()
            gs[parts_g(P1C1)[0][0]] = (hold[P1C1] + g3[2].astype(F32)).astype(BF16)
            send_g(P1C1)

    for i in range(6):
        q, kind = CHUNK[i], KIND[i]
        for early in ((), (P3C0,), (P2C0,), (P3C1, P2C1), (), ())[i]:
            pass_w(early)
        if i == 2:
            finish_z(P1C1)
        if i == 4:
            pass_g(P3C0)
            finish_p1(0)
        if i == 5:
            finish_z(P3C1)
            pass_g(P2C0)
        for copy in whole_w(i, 4 + i):
            copy.wait_recv()
        if i == 0:
            send_w(P3C0, 4 + i)
        if i == 1:
            send_w(P2C0, 0)
            send_w(P3C1, 4 + i)
            send_w(P2C1, 1)
        compute(4 + i, 0, 1 if kind == 3 else 2)
        if i == P1C0:
            p1full[...] = grad[...]
        elif q == 0:
            send_whole(i)
        else:
            hold[i] = my_half(grad, rep)
            zs[i] = my_half(grad, orep).astype(BF16)
            swap_z(i).start()

    outs = [
        remote(acc.at[other], orecv.at[a], out_send.at[a], out_recv.at[a], peer)
        for a, acc in enumerate((facc, iacc))
    ]
    for copy in outs:
        copy.start()
    pass_g(P1C0)
    merge_own(0)
    finish_z(P2C1)
    pass_g(P3C1)
    finish_p1(1)
    merge_own(1)
    pass_g(P2C1)
    pass_g(P1C1)

    for a, (acc, out) in enumerate(((facc, fout), (iacc, iout))):
        outs[a].wait_recv()
        out[...] = (acc[core] + orecv[a]).astype(BF16)

    def arrived(slot, core_, q):
        ref = final.at[slot, core_, q]
        remote(ref, ref, z_send.at[0], fin_sem.at[slot, core_, q], ahead).wait_recv()
        return ref[...].astype(F32)

    def finish(q):
        for core_ in (core, other):
            total = keep[q] if core_ is core else arrived(rep, core_, q)
            total = total + arrived(orep, core_, q)
            if q == 1:
                total = total + arrived(2, core_, q)
            at_hid = pl.multiple_of(core_ * HALF + q * CH, CH)
            inout[:, pl.ds(at_hid, CH)] = total[0].T
            downout[pl.ds(at_hid, CH), :] = total[1]

    finish(0)
    finish(1)

    for copy in swaps + swap_t + outs:
        copy.wait_send()
    for i in range(6):
        sent_w(i)
        passed_w(i)
        passed_g(i)
        for slot, _, _, _ in parts_g(i):
            remote(gs.at[slot], gs.at[slot], xm_send.at[slot], g3_sem.at[0], ahead).wait_send()
        if CHUNK[i] == 1:
            swap_z(i).wait_send()
    for n in range(4):
        for h in range(2):
            @pl.when(jnp.logical_not((core == n // 2) & (rep == h)))
            def _():
                own_copy(n, h).wait_send()


def hand_on(a, b, c, d, ao, bo, co, do):
    for src, dst in ((a, ao), (b, bo), (c, co), (d, do)):
        dst[...] = src[...]


def on_device(fwd_in, bwd_in, cotangent, w_in, w_out):
    dma = pltpu.SemaphoreType.DMA
    vmem = pltpu.VMEM
    results = pl.pallas_call(
        kernel,
        out_shape=(
            jax.ShapeDtypeStruct((MB, D), BF16),
            jax.ShapeDtypeStruct((MB, D), BF16),
            jax.ShapeDtypeStruct((HID, HID), F32),
            jax.ShapeDtypeStruct((HID, HID), F32),
        ),
        in_specs=[pl.BlockSpec(memory_space=pl.ANY)] * 5,
        out_specs=[pl.BlockSpec(memory_space=pltpu.VMEM)] * 4,
        scratch_shapes=[
            vmem((3, 2, MB, D), BF16),
            vmem((10, D, CH), BF16),
            vmem((10, CH, D), BF16),
            vmem((2, MB, D), F32),
            vmem((2, MB, D), F32),
            vmem((2, MB, D), F32),
            vmem((2, CH, D), F32),
            vmem((4, 2, 2, CH, 512), BF16),
            vmem((9, 2, CH, 512), BF16),
            vmem((6, 2, CH, 512), F32),
            vmem((6, 2, CH, 512), BF16),
            vmem((6, 2, CH, 512), BF16),
            vmem((2, 2, CH, 512), F32),
            vmem((3, 2, 2, 2, CH, 512), BF16),
            vmem((3, 2, CH, 512), BF16),
            vmem((2, CH, D), F32),
            vmem((2, 2, CH, D), F32),
            vmem((2, 2, 2, CH, 512), BF16),
            vmem((6, 512, CH), BF16),
            vmem((6, 64, D), BF16),
            vmem((9, 96, 512), BF16),
            dma((7,)),
            dma((2, 2)),
            dma((2, 2)),
            dma((3,)),
            dma((3,)),
            dma((6, 2)),
            dma((6, 2)),
            dma((6,)),
            dma((6, 2, 2)),
            dma((6, 2)),
            dma((4, 2)),
            dma((3, 2, 2)),
            dma((9,)),
            dma((2,)),
            dma((6,)),
            dma((6,)),
            dma((9,)),
            dma((9,)),
            dma((2,)),
            dma((2,)),
            dma((2,)),
        ],
        compiler_params=pltpu.CompilerParams(
            collective_id=0, has_side_effects=True, vmem_limit_bytes=60 * 2**20
        ),
        cost_estimate=pl.CostEstimate(
            flops=13_153_337_344, bytes_accessed=12 * 2**20, transcendentals=2 * 4 * MB * HID
        ),
    )(fwd_in, bwd_in, cotangent, w_in, w_out)
    steps = 2
    blocks = [
        pl.BlockSpec((r.shape[0] // steps, r.shape[1]), lambda step: (step, 0)) for r in results
    ]
    return pl.pallas_call(
        hand_on,
        grid=(steps,),
        out_shape=tuple(jax.ShapeDtypeStruct(r.shape, r.dtype) for r in results),
        in_specs=blocks,
        out_specs=blocks,
        compiler_params=pltpu.CompilerParams(vmem_limit_bytes=60 * 2**20),
    )(*results)


def solution(mesh):
    in_specs = (
        P(("blk", "rep"), None),
        P(("blk", "rep"), None),
        P(("blk", "rep"), None),
        P(None, "blk"),
        P("blk", None),
    )
    out_specs = (P(("blk", "rep"), None), P(("blk", "rep"), None), P("rep", "blk"), P("blk", "rep"))
    return jax.shard_map(
        on_device, mesh=mesh, in_specs=in_specs, out_specs=out_specs, check_vma=False
    )
```
